32 devices in a mesh: groups: 2 (over x), seq: 16 (over z, y, core).
Axes of the slice: x: 2, y: 2, z: 4, core: 2. Of those that a mesh axis runs over, the one named last changes fastest.
Arguments:
- queries: bfloat16 [8192, 2048], P(('groups', 'seq')), parts along dimension 0, may hold values from -9 to 9
- keys: bfloat16 [8192, 512], P(('groups', 'seq')), parts along dimension 0, may hold values from -9 to 9
- values: bfloat16 [8192, 512], P(('groups', 'seq')), parts along dimension 0, may hold values from -6 to 6
- segment: int32 [8192], P(('groups', 'seq')), parts along dimension 0, may hold values from 0 to 10, never falling along the last dimension, each value on 1 to 769 neighbouring positions
- out_weight: bfloat16 [2048, 4096], P('seq'), may hold values from -0.125 to 0.125
Outputs:
- projected: bfloat16 [8192, 4096], P(('groups', 'seq')), parts along dimension 0
The draws below stay inside these ranges and needn't reach their ends.
There are 2 independent parts, one for each index of `groups`. The reference program is written for one: setup_inputs(seed, part) draws one part's arguments, and reference() takes and returns one part's arrays. A program takes and returns all parts, laid end to end along the dimension named above; an argument that names none is the same for every part. Nothing has to cross between parts.
Inputs may be any that keep to these rules, and one draw needn't show every extreme that they name: `segment`: document numbers never fall along the stretch; every document has 1 to 769 tokens.
All inputs are finite; a program needn't handle non-finite values.
Results may differ from the reference program's by a relative error of at most 0.0053.
Values may be sent and summed in bfloat16 or wider, within the bound.
A program may use at most 128 MiB of HBM per device.

```python
import math
import jax
import jax.numpy as jnp
import numpy as np
from jax import lax

D = 4096
HEADS = 16
KV_HEADS = 4
HEAD = 128
TOK_DEV = 256
SPAN = 4
MOST = 769
TOKENS = 4096
DOCS = 11
N_SEQ = 16


def draw_queries(key, part):
    shape_four = (TOKENS, KV_HEADS, HEADS // KV_HEADS, HEAD)
    base_draw = jnp.clip(jax.random.normal(jax.random.fold_in(key, 1), shape_four, jnp.float32), -4.0, 4.0)
    return base_draw.reshape(TOKENS, HEADS * HEAD).astype(jnp.bfloat16)


def draw_keys(key, part):
    shape_three = (TOKENS, KV_HEADS, HEAD)
    base_draw = jnp.clip(jax.random.normal(jax.random.fold_in(key, 2), shape_three, jnp.float32), -4.0, 4.0)
    return base_draw.reshape(TOKENS, KV_HEADS * HEAD).astype(jnp.bfloat16)


def block_scale(key, extent, cuts, low, high):
    gain, own = 1.0, jax.random.fold_in(key, 6)
    for position, shards_of in cuts:
        heights = jnp.exp(jax.random.uniform(jax.random.fold_in(own, position), (shards_of,), jnp.float32, low / len(cuts), high / len(cuts)))
        gain = gain * jnp.repeat(heights, extent[position] // shards_of).reshape([-1 if axis == position else 1 for axis in range(len(extent))])
    return gain


def split_up(number_of, total, bound, slope):
    weights = [(1 << 20) // math.isqrt(rank ** slope) + 1 for rank in range(2, number_of + 1)]
    surplus, holding = total - bound - (number_of - 1), [1] * (number_of - 1)
    while surplus > 0:
        free = [i for i in range(number_of - 1) if holding[i] < bound]
        whole, remaining = sum([weights[i] for i in free]), surplus
        for i in free:
            addition = min(bound - holding[i], max(1, remaining * weights[i] // whole), surplus)
            holding[i] = holding[i] + addition
            surplus = surplus - addition
    return np.array([bound] + holding)


def ragged(key, amount, total, most, lean):
    if amount == 2:
        one = jax.random.randint(key, (), max(1, total - most), min(most, total - 1) + 1)
        return jnp.stack([one, total - one])
    sizes = jnp.asarray(split_up(amount, total, most, lean), jnp.int32)
    couples = (amount - 1) // 2
    donor, taker = sizes[1:1 + 2 * couples:2], sizes[2:2 + 2 * couples:2]
    room = jnp.minimum(donor - 1, most - taker)
    moved = jax.random.randint(jax.random.fold_in(key, 1), (couples,), 0, 1 << 20) % (room + 1)
    sizes = sizes.at[1:1 + 2 * couples:2].set(donor - moved).at[2:2 + 2 * couples:2].set(taker + moved)
    return sizes[jax.random.permutation(jax.random.fold_in(key, 2), amount)]


def gaussian(own_key, shape, width, most, pieces=(), kind=jnp.bfloat16):
    gain = block_scale(own_key, shape, pieces, -0.22, 0.18) if pieces else 1.0
    values = jax.random.normal(own_key, shape, jnp.float32) * width * gain
    return jnp.minimum(jnp.maximum(values, -most), most).astype(kind)


def setup_inputs(seed: int = 0, part: int = 0) -> dict:
    key_list = jax.random.split(jax.random.key(seed), 6)
    part_splits = jax.random.split(jax.random.fold_in(key_list[5], part), 6)
    queries = draw_queries(jax.random.fold_in(jax.random.fold_in(key_list[5], part), 71), part)
    keys = draw_keys(jax.random.fold_in(jax.random.fold_in(key_list[5], part), 71), part)
    values = gaussian(part_splits[2], (TOKENS, KV_HEADS * HEAD), 1.0, 6.0, ((0, 16),))
    segment = jnp.searchsorted(jnp.cumsum(ragged(part_splits[3], DOCS, TOKENS, MOST, 1)), jnp.arange(TOKENS), side="right").astype(jnp.int32)
    out_weight = gaussian(key_list[4], (HEADS * HEAD, D), (HEADS * HEAD) ** -0.5, 0.125, ((0, 16),))
    return dict(queries=queries, keys=keys, values=values, segment=segment, out_weight=out_weight)


def one_head(query_group, key_head, value_head, live_mask):
    scores = jnp.einsum("thd,sd->ths", query_group.astype(jnp.float32), key_head.astype(jnp.float32)) * (HEAD ** -0.5)
    scores = jnp.where(live_mask[:, None, :], scores, -jnp.inf)
    row_max = jnp.max(scores, axis=-1, keepdims=True)
    weights = jnp.exp(scores - row_max)
    weight_sum = jnp.sum(weights, axis=-1, keepdims=True)
    probabilities = weights.astype(jnp.bfloat16)
    head_mix = jnp.einsum("ths,sd->thd", probabilities.astype(jnp.float32), value_head.astype(jnp.float32))
    return head_mix / weight_sum


def attend(queries_block, keys_window, values_window, live_mask):
    row_count = queries_block.shape[0]
    window_rows = keys_window.shape[0]
    group_size = HEADS // KV_HEADS
    query_heads = queries_block.reshape(row_count, KV_HEADS, group_size, HEAD).transpose(1, 0, 2, 3)
    key_heads = keys_window.reshape(window_rows, KV_HEADS, HEAD).transpose(1, 0, 2)
    value_heads = values_window.reshape(window_rows, KV_HEADS, HEAD).transpose(1, 0, 2)

    def per_group(operands):
        return one_head(operands[0], operands[1], operands[2], live_mask)

    head_outputs = lax.map(per_group, (query_heads, key_heads, value_heads))
    return head_outputs.transpose(1, 0, 2, 3).reshape(row_count, HEADS * HEAD).astype(jnp.bfloat16)


def reference(queries, keys, values, segment, out_weight):
    pad_rows = (SPAN - 1) * TOK_DEV
    keys_padded = jnp.concatenate([jnp.zeros((pad_rows, keys.shape[1]), keys.dtype), keys], axis=0)
    values_padded = jnp.concatenate([jnp.zeros((pad_rows, values.shape[1]), values.dtype), values], axis=0)
    segment_padded = jnp.concatenate([jnp.full((pad_rows,), -1, jnp.int32), segment.astype(jnp.int32)], axis=0)

    def per_block(block_id):
        first_row = (block_id * TOK_DEV).astype(jnp.int32)
        queries_block = lax.dynamic_slice_in_dim(queries, first_row, TOK_DEV, 0)
        keys_window = lax.dynamic_slice_in_dim(keys_padded, first_row, SPAN * TOK_DEV, 0)
        values_window = lax.dynamic_slice_in_dim(values_padded, first_row, SPAN * TOK_DEV, 0)
        segment_query = lax.dynamic_slice_in_dim(segment.astype(jnp.int32), first_row, TOK_DEV, 0)
        segment_key = lax.dynamic_slice_in_dim(segment_padded, first_row, SPAN * TOK_DEV, 0)
        query_pos = first_row + jnp.arange(TOK_DEV, dtype=jnp.int32)
        key_pos = first_row - pad_rows + jnp.arange(SPAN * TOK_DEV, dtype=jnp.int32)
        live_mask = (segment_query[:, None] == segment_key[None, :]) & (key_pos[None, :] <= query_pos[:, None])
        attention = attend(queries_block, keys_window, values_window, live_mask)
        return jnp.dot(attention, out_weight, preferred_element_type=jnp.float32).astype(jnp.bfloat16)

    blocks = lax.map(per_block, jnp.arange(N_SEQ, dtype=jnp.int32))
    return blocks.reshape(TOKENS, out_weight.shape[1])
```

```python
import functools
import math

import jax
import jax.numpy as jnp
from jax import lax
from jax.experimental import pallas as pl
from jax.experimental.pallas import tpu as pltpu
from jax.sharding import PartitionSpec as P

HEADS = 16
KV_HEADS = 4
HEAD = 128
SPAN = 4
CORES = 2
UP_A, DOWN_A, UP_B, DOWN_B, ACROSS, SIBLING = range(6)


def grid_of(n):
    chips = n // CORES
    b = max(d for d in range(1, chips + 1) if chips % d == 0 and d * d <= chips)
    return chips // b, b


def kernel(n, A, B, wx, tile,
           q_ref, k_ref, v_ref, seg_row_ref, seg_col_ref, w_ref, out_ref,
           W, kwin, vwin, swin, bias, att,
           send, recv, kv_send, kv_recv):
    rows = q_ref.shape[0]
    depth = w_ref.shape[0]
    width = w_ref.shape[1]
    g = lax.axis_index("groups")
    i = lax.axis_index("seq")
    c = lax.rem(i, CORES)
    chip = i // CORES
    b = lax.rem(chip, B)
    a = chip // B

    def index(a_, b_, c_):
        return (a_ * B + b_) * CORES + c_

    widths = (wx, width - 2 * wx, wx)
    starts = (g * wx, 2 * wx, (1 - g) * wx)
    number = (g, 2, 1 - g)

    def move(p, s, way, device):
        view = W.at[pl.ds(pl.multiple_of(s * depth, depth), depth),
                    pl.ds(pl.multiple_of(starts[p], 128), widths[p])]
        return pltpu.make_async_remote_copy(
            src_ref=view, dst_ref=view,
            send_sem=send.at[way, p, s], recv_sem=recv.at[number[p], s],
            device_id=device, device_id_type=pl.DeviceIdType.MESH)

    def act(copy, mode):
        if mode == "start":
            copy.start()
        else:
            copy.wait_send()

    up_a = (g, index(a + 1, b, c))
    down_a = (g, index(a - 1, b, c))
    up_b = (g, index(a, b + 1, c))
    down_b = (g, index(a, b - 1, c))
    across = (1 - g, i)
    sibling = (g, index(a, b, 1 - c))

    def along_b(p, s, mode):
        pl.when(b + 1 < B)(lambda: act(move(p, s, UP_B, up_b), mode))
        pl.when(b > 0)(lambda: act(move(p, s, DOWN_B, down_b), mode))

    def arrive(p, s, mode):
        if mode == "start":
            move(p, s, SIBLING, sibling).wait_recv()

    def own(mode):
        for p in (0, 1):
            pl.when(a + 1 < A)(lambda: act(move(p, i, UP_A, up_a), mode))
            pl.when(a > 0)(lambda: act(move(p, i, DOWN_A, down_a), mode))
            along_b(p, i, mode)
        for p in (0, 1, 2):
            act(move(p, i, SIBLING, sibling), mode)

    def from_a(p, t, mode):
        def take(a_, way, device, more):
            s = index(a_, b, c)
            arrive(p, s, mode)
            pl.when(more)(lambda: act(move(p, s, way, device), mode))
            along_b(p, s, mode)
            if p == 0:
                act(move(p, s, ACROSS, across), mode)
            act(move(p, s, SIBLING, sibling), mode)

        pl.when(a - t >= 0)(lambda: take(a - t, UP_A, up_a, a + 1 < A))
        pl.when(a + t < A)(lambda: take(a + t, DOWN_A, down_a, a > 0))

    def from_b(p, t, mode):
        def take(a_, b_, way, device, more):
            s = index(a_, b_, c)
            arrive(p, s, mode)
            pl.when(more)(lambda: act(move(p, s, way, device), mode))
            if p == 0:
                act(move(p, s, ACROSS, across), mode)
            act(move(p, s, SIBLING, sibling), mode)

        def column(a_):
            def step(u, carry):
                pl.when(b - u >= 0)(lambda: take(a_, b - u, UP_B, up_b, b + 1 < B))
                pl.when(b + u < B)(lambda: take(a_, b + u, DOWN_B, down_b, b > 0))
                return carry

            lax.fori_loop(1, B, step, 0)

        if t == 0:
            column(a)
        else:
            pl.when(a - t >= 0)(lambda: column(a - t))
            pl.when(a + t < A)(lambda: column(a + t))

    def from_across(t, mode):
        def column(a_):
            def step(b_, carry):
                s = index(a_, b_, c)

                @pl.when(s != i)
                def _():
                    arrive(2, s, mode)
                    act(move(2, s, SIBLING, sibling), mode)

                return carry

            lax.fori_loop(0, B, step, 0)

        if t == 0:
            column(a)
        else:
            pl.when(a - t >= 0)(lambda: column(a - t))
            pl.when(a + t < A)(lambda: column(a + t))

    def kv_copies(d):
        to = (g, lax.rem(i + d, n))
        mine, theirs = SPAN - 1, SPAN - 1 - d
        return [
            pltpu.make_async_remote_copy(
                src_ref=ref.at[mine], dst_ref=ref.at[theirs],
                send_sem=kv_send.at[d - 1, m], recv_sem=kv_recv.at[d - 1, m],
                device_id=to, device_id_type=pl.DeviceIdType.MESH)
            for m, ref in enumerate((kwin, vwin, swin))]

    barrier = pltpu.get_barrier_semaphore()

    def greet(device):
        pl.semaphore_signal(barrier, inc=1, device_id=device,
                            device_id_type=pl.DeviceIdType.MESH)

    pl.when(a + 1 < A)(lambda: greet(up_a))
    pl.when(a > 0)(lambda: greet(down_a))
    pl.when(b + 1 < B)(lambda: greet(up_b))
    pl.when(b > 0)(lambda: greet(down_b))
    greet(across)
    greet(sibling)
    for d in range(1, SPAN):
        greet((g, lax.rem(i + d, n)))
        greet((g, lax.rem(i + n - d, n)))
    W[pl.ds(pl.multiple_of(i * depth, depth), depth), :] = w_ref[...]
    kwin[SPAN - 1] = k_ref[...]
    vwin[SPAN - 1] = v_ref[...]
    swin[SPAN - 1] = seg_row_ref[...]
    expected = (2 + 2 * (SPAN - 1)
                + jnp.where(a + 1 < A, 1, 0) + jnp.where(a > 0, 1, 0)
                + jnp.where(b + 1 < B, 1, 0) + jnp.where(b > 0, 1, 0))
    pl.semaphore_wait(barrier, expected)

    for d in range(1, SPAN):
        for copy in kv_copies(d):
            copy.start()
    own("start")
    for d in range(1, SPAN):
        for copy in kv_copies(d):
            copy.wait_recv()

    for j in range(SPAN):
        row = lax.broadcasted_iota(jnp.int32, (rows, rows), 0)
        col = lax.broadcasted_iota(jnp.int32, (rows, rows), 1) + (j - SPAN + 1) * rows
        live = (seg_col_ref[:, 0:1] == swin[j, 0:1, :]) & (col <= row) & (col + i * rows >= 0)
        bias[:, j * rows:(j + 1) * rows] = jnp.where(live, 0.0, -jnp.inf)

    factor = HEAD ** -0.5 * math.log2(math.e)
    group = HEADS // KV_HEADS

    def attend(kv):
        lanes = slice(kv * HEAD, (kv + 1) * HEAD)
        keys = jnp.concatenate([kwin[j, :, lanes] for j in range(SPAN)], axis=0)
        vals = jnp.concatenate([vwin[j, :, lanes] for j in range(SPAN)], axis=0)
        for m in range(group):
            h = kv * group + m
            q = q_ref[:, h * HEAD:(h + 1) * HEAD]
            scores = lax.dot_general(q, keys, (((1,), (1,)), ((), ())),
                                     preferred_element_type=jnp.float32)
            scores = scores * factor + bias[...]
            top = jnp.max(scores, axis=-1, keepdims=True)
            weights = jnp.exp2(scores - top)
            total = jnp.sum(weights, axis=-1, keepdims=True)
            mix = jnp.dot(weights.astype(jnp.bfloat16), vals,
                          preferred_element_type=jnp.float32)
            att[:, h * HEAD:(h + 1) * HEAD] = (mix / total).astype(jnp.bfloat16)

    done = 0
    for t in range(A):
        if t > 0:
            from_a(0, t, "start")
        from_b(0, t, "start")
        if t > 0:
            from_a(1, t, "start")
        from_b(1, t, "start")
        if t > 1:
            from_across(t - 2, "start")
        if done < KV_HEADS:
            attend(done)
            done += 1
    for kv in range(done, KV_HEADS):
        attend(kv)

    def project(p):
        def landed(m, carry):
            move(p, m * CORES + 1 - c, SIBLING, sibling).wait_recv()
            return carry

        lax.fori_loop(0, n // CORES, landed, 0)

        def one(m, carry):
            lanes = pl.ds(pl.multiple_of(starts[p] + m * tile, 128), tile)
            out_ref[:, lanes] = jnp.dot(
                att[...], W[:, lanes], preferred_element_type=jnp.float32
            ).astype(out_ref.dtype)
            return carry

        lax.fori_loop(0, widths[p] // tile, one, 0)

    project(0)
    for t in range(max(A - 2, 0), A):
        from_across(t, "start")
    project(1)
    project(2)

    own("wait")
    for t in range(A):
        for p in (0, 1):
            if t > 0:
                from_a(p, t, "wait")
            from_b(p, t, "wait")
        from_across(t, "wait")
    for d in range(1, SPAN):
        for copy in kv_copies(d):
            copy.wait_send()


def body(queries, keys, values, segment, out_weight):
    rows, q_width = queries.shape
    kv_width = keys.shape[1]
    n = lax.axis_size("seq")
    width = out_weight.shape[1]
    A, B = grid_of(n)
    tile = math.gcd(width, 512)
    wx = width * 3 // 8 // tile * tile
    seg_row = jnp.broadcast_to(segment[None, :], (8, rows))
    seg_col = jnp.broadcast_to(segment[:, None], (rows, 128))
    vmem = pl.BlockSpec(memory_space=pltpu.VMEM)
    window = rows * SPAN
    return pl.pallas_call(
        functools.partial(kernel, n, A, B, wx, tile),
        out_shape=jax.ShapeDtypeStruct((rows, width), jnp.bfloat16),
        in_specs=[vmem] * 6,
        out_specs=vmem,
        scratch_shapes=[
            pltpu.VMEM((out_weight.shape[0] * n, width), jnp.bfloat16),
            pltpu.VMEM((SPAN, rows, kv_width), jnp.bfloat16),
            pltpu.VMEM((SPAN, rows, kv_width), jnp.bfloat16),
            pltpu.VMEM((SPAN, 8, rows), jnp.int32),
            pltpu.VMEM((rows, window), jnp.float32),
            pltpu.VMEM((rows, q_width), jnp.bfloat16),
            pltpu.SemaphoreType.DMA((6, 3, n)),
            pltpu.SemaphoreType.DMA((3, n)),
            pltpu.SemaphoreType.DMA((SPAN - 1, 3)),
            pltpu.SemaphoreType.DMA((SPAN - 1, 3)),
        ],
        compiler_params=pltpu.CompilerParams(
            collective_id=0, has_side_effects=True, vmem_limit_bytes=56 * 2**20),
        cost_estimate=pl.CostEstimate(
            flops=2 * rows * q_width * (2 * window + width),
            bytes_accessed=4 * rows * width, transcendentals=rows * window * HEADS),
    )(queries, keys, values, seg_row, seg_col, out_weight)


def solution(mesh):
    in_specs = (
        P(("groups", "seq"), None),
        P(("groups", "seq"), None),
        P(("groups", "seq"), None),
        P(("groups", "seq")),
        P("seq", None),
    )
    out_specs = P(("groups", "seq"), None)
    return jax.shard_map(body, mesh=mesh, in_specs=in_specs, out_specs=out_specs, check_vma=False)
```

```python
import functools
import math

import jax
import jax.numpy as jnp
from jax import lax
from jax.experimental import pallas as pl
from jax.experimental.pallas import tpu as pltpu
from jax.sharding import PartitionSpec as P

HEADS = 16
KV_HEADS = 4
HEAD = 128
SPAN = 4
CORES = 2
UP_A, DOWN_A, UP_B, DOWN_B, ACROSS, SIBLING = range(6)


def grid_of(n):
    chips = n // CORES
    b = max(d for d in range(1, chips + 1) if chips % d == 0 and d * d <= chips)
    return chips // b, b


def kernel(n, A, B, wx, cuts, tile,
           q_ref, k_ref, v_ref, seg_row_ref, seg_col_ref, w_ref, out_ref,
           W, kwin, vwin, swin, bias, att,
           send, recv, kv_send, kv_recv):
    rows = q_ref.shape[0]
    depth = w_ref.shape[0]
    width = w_ref.shape[1]
    g = lax.axis_index("groups")
    i = lax.axis_index("seq")
    c = lax.rem(i, CORES)
    chip = i // CORES
    b = lax.rem(chip, B)
    a = chip // B

    def index(a_, b_, c_):
        return (a_ * B + b_) * CORES + c_

    part = wx // cuts
    rest = width - 2 * wx
    MINE = tuple(range(cuts))
    BOTH = (cuts,)
    THEIRS = tuple(range(cuts + 1, 2 * cuts + 1))
    widths = (part,) * cuts + (rest,) + (part,) * cuts
    starts = (tuple(g * wx + j * part for j in range(cuts)) + (2 * wx,)
              + tuple((1 - g) * wx + j * part for j in range(cuts)))
    number = (tuple(g * cuts + j for j in range(cuts)) + (2 * cuts,)
              + tuple((1 - g) * cuts + j for j in range(cuts)))

    def move(p, s, way, device):
        view = W.at[pl.ds(pl.multiple_of(s * depth, depth), depth),
                    pl.ds(pl.multiple_of(starts[p], 128), widths[p])]
        return pltpu.make_async_remote_copy(
            src_ref=view, dst_ref=view,
            send_sem=send.at[way, p, s], recv_sem=recv.at[number[p], s],
            device_id=device, device_id_type=pl.DeviceIdType.MESH)

    def act(copy, mode):
        if mode == "start":
            copy.start()
        else:
            copy.wait_send()

    up_a = (g, index(a + 1, b, c))
    down_a = (g, index(a - 1, b, c))
    up_b = (g, index(a, b + 1, c))
    down_b = (g, index(a, b - 1, c))
    across = (1 - g, i)
    sibling = (g, index(a, b, 1 - c))

    def along_b(p, s, mode):
        pl.when(b + 1 < B)(lambda: act(move(p, s, UP_B, up_b), mode))
        pl.when(b > 0)(lambda: act(move(p, s, DOWN_B, down_b), mode))

    def arrive(p, s, mode):
        if mode == "start":
            move(p, s, SIBLING, sibling).wait_recv()

    def own(pieces, mode):
        for p in pieces:
            pl.when(a + 1 < A)(lambda: act(move(p, i, UP_A, up_a), mode))
            pl.when(a > 0)(lambda: act(move(p, i, DOWN_A, down_a), mode))
            along_b(p, i, mode)
            act(move(p, i, SIBLING, sibling), mode)

    def from_a(p, t, mode):
        def take(a_, way, device, more):
            s = index(a_, b, c)
            arrive(p, s, mode)
            pl.when(more)(lambda: act(move(p, s, way, device), mode))
            along_b(p, s, mode)
            if p in MINE:
                act(move(p, s, ACROSS, across), mode)
            act(move(p, s, SIBLING, sibling), mode)

        pl.when(a - t >= 0)(lambda: take(a - t, UP_A, up_a, a + 1 < A))
        pl.when(a + t < A)(lambda: take(a + t, DOWN_A, down_a, a > 0))

    def from_b(p, t, mode):
        def take(a_, b_, way, device, more):
            s = index(a_, b_, c)
            arrive(p, s, mode)
            pl.when(more)(lambda: act(move(p, s, way, device), mode))
            if p in MINE:
                act(move(p, s, ACROSS, across), mode)
            act(move(p, s, SIBLING, sibling), mode)

        def column(a_):
            def step(u, carry):
                pl.when(b - u >= 0)(lambda: take(a_, b - u, UP_B, up_b, b + 1 < B))
                pl.when(b + u < B)(lambda: take(a_, b + u, DOWN_B, down_b, b > 0))
                return carry

            lax.fori_loop(1, B, step, 0)

        if t == 0:
            column(a)
        else:
            pl.when(a - t >= 0)(lambda: column(a - t))
            pl.when(a + t < A)(lambda: column(a + t))

    def from_across(p, t, mode):
        def column(a_):
            def step(b_, carry):
                s = index(a_, b_, c)

                @pl.when(s != i)
                def _():
                    arrive(p, s, mode)
                    act(move(p, s, SIBLING, sibling), mode)

                return carry

            lax.fori_loop(0, B, step, 0)

        if t == 0:
            column(a)
        else:
            pl.when(a - t >= 0)(lambda: column(a - t))
            pl.when(a + t < A)(lambda: column(a + t))

    last = SPAN - 1
    routes = ((last, 1, (g, lax.rem(i + 2, n))),
              (1, 2 * c, sibling),
              (last, 2 - 2 * c, (g, lax.rem(i + 1 + 2 * c, n))))

    def kv_copies(way):
        mine, theirs, to = routes[way]
        return [
            pltpu.make_async_remote_copy(
                src_ref=ref.at[mine], dst_ref=ref.at[theirs],
                send_sem=kv_send.at[way, m], recv_sem=kv_recv.at[theirs, m],
                device_id=to, device_id_type=pl.DeviceIdType.MESH)
            for m, ref in enumerate((kwin, vwin, swin))]

    barrier = pltpu.get_barrier_semaphore()

    def greet(device):
        pl.semaphore_signal(barrier, inc=1, device_id=device,
                            device_id_type=pl.DeviceIdType.MESH)

    pl.when(a + 1 < A)(lambda: greet(up_a))
    pl.when(a > 0)(lambda: greet(down_a))
    pl.when(b + 1 < B)(lambda: greet(up_b))
    pl.when(b > 0)(lambda: greet(down_b))
    greet(across)
    greet(sibling)
    for d in range(1, SPAN):
        greet((g, lax.rem(i + d, n)))
        greet((g, lax.rem(i + n - d, n)))
    W[pl.ds(pl.multiple_of(i * depth, depth), depth), :] = w_ref[...]
    kwin[SPAN - 1] = k_ref[...]
    vwin[SPAN - 1] = v_ref[...]
    swin[SPAN - 1] = seg_row_ref[...]
    expected = (2 + 2 * (SPAN - 1)
                + jnp.where(a + 1 < A, 1, 0) + jnp.where(a > 0, 1, 0)
                + jnp.where(b + 1 < B, 1, 0) + jnp.where(b > 0, 1, 0))
    pl.semaphore_wait(barrier, expected)

    own(MINE, "start")
    for way in (0, 2):
        for copy in kv_copies(way):
            copy.start()
    own(BOTH, "start")
    for p in THEIRS:
        move(p, i, SIBLING, sibling).start()

    def slot(j):
        return [
            pltpu.make_async_remote_copy(
                src_ref=ref.at[last], dst_ref=ref.at[j],
                send_sem=kv_send.at[0, m], recv_sem=kv_recv.at[j, m],
                device_id=sibling, device_id_type=pl.DeviceIdType.MESH)
            for m, ref in enumerate((kwin, vwin, swin))]

    def mask():
        for j in range(SPAN):
            row = lax.broadcasted_iota(jnp.int32, (rows, rows), 0)
            col = lax.broadcasted_iota(jnp.int32, (rows, rows), 1) + (j - SPAN + 1) * rows
            live = (seg_col_ref[:, 0:1] == swin[j, 0:1, :]) & (col <= row) & (col + i * rows >= 0)
            bias[:, j * rows:(j + 1) * rows] = jnp.where(live, 0.0, -jnp.inf)

    factor = HEAD ** -0.5 * math.log2(math.e)
    group = HEADS // KV_HEADS

    def attend(kv):
        lanes = slice(kv * HEAD, (kv + 1) * HEAD)
        keys = jnp.concatenate([kwin[j, :, lanes] for j in range(SPAN)], axis=0)
        vals = jnp.concatenate([vwin[j, :, lanes] for j in range(SPAN)], axis=0)
        for m in range(group):
            h = kv * group + m
            q = q_ref[:, h * HEAD:(h + 1) * HEAD]
            scores = lax.dot_general(q, keys, (((1,), (1,)), ((), ())),
                                     preferred_element_type=jnp.float32)
            scores = scores * factor + bias[...]
            top = jnp.max(scores, axis=-1, keepdims=True)
            weights = jnp.exp2(scores - top)
            total = jnp.sum(weights, axis=-1, keepdims=True)
            mix = jnp.dot(weights.astype(jnp.bfloat16), vals,
                          preferred_element_type=jnp.float32)
            att[:, h * HEAD:(h + 1) * HEAD] = (mix / total).astype(jnp.bfloat16)

    done = 0
    for t in range(A):
        for p in MINE + BOTH:
            if t > 0:
                from_a(p, t, "start")
            from_b(p, t, "start")
        if t == 0:
            for copy in slot(1):
                copy.wait_recv()
            for copy in kv_copies(1):
                copy.start()
        if t == 1:
            for j in (0, 2):
                for copy in slot(j):
                    copy.wait_recv()
            mask()
        if t > 0:
            for p in THEIRS:
                from_across(p, t - 1, "start")
            if done < KV_HEADS:
                attend(done)
                done += 1
    for kv in range(done, KV_HEADS):
        attend(kv)

    def project(p):
        def landed(m, carry):
            move(p, m * CORES + 1 - c, SIBLING, sibling).wait_recv()
            return carry

        lax.fori_loop(0, n // CORES, landed, 0)

        def one(m, carry):
            lanes = pl.ds(pl.multiple_of(starts[p] + m * tile, 128), tile)
            out_ref[:, lanes] = jnp.dot(
                att[...], W[:, lanes], preferred_element_type=jnp.float32
            ).astype(out_ref.dtype)
            return carry

        lax.fori_loop(0, widths[p] // tile, one, 0)

    for p in MINE:
        project(p)
    for p in THEIRS:
        from_across(p, A - 1, "start")
    for p in BOTH + THEIRS:
        project(p)

    own(MINE + BOTH, "wait")
    for p in THEIRS:
        move(p, i, SIBLING, sibling).wait_send()
    for t in range(A):
        for p in MINE + BOTH:
            if t > 0:
                from_a(p, t, "wait")
            from_b(p, t, "wait")
        for p in THEIRS:
            from_across(p, t, "wait")
    for way in range(3):
        for copy in kv_copies(way):
            copy.wait_send()


def body(queries, keys, values, segment, out_weight):
    rows, q_width = queries.shape
    kv_width = keys.shape[1]
    n = lax.axis_size("seq")
    width = out_weight.shape[1]
    A, B = grid_of(n)
    tile = math.gcd(width, 512)
    cuts = 1
    wx = width * 3 // 8 // (cuts * tile) * (cuts * tile)
    seg_row = jnp.broadcast_to(segment[None, :], (8, rows))
    seg_col = jnp.broadcast_to(segment[:, None], (rows, 128))
    vmem = pl.BlockSpec(memory_space=pltpu.VMEM)
    window = rows * SPAN
    return pl.pallas_call(
        functools.partial(kernel, n, A, B, wx, cuts, tile),
        out_shape=jax.ShapeDtypeStruct((rows, width), jnp.bfloat16),
        in_specs=[vmem] * 6,
        out_specs=vmem,
        scratch_shapes=[
            pltpu.VMEM((out_weight.shape[0] * n, width), jnp.bfloat16),
            pltpu.VMEM((SPAN, rows, kv_width), jnp.bfloat16),
            pltpu.VMEM((SPAN, rows, kv_width), jnp.bfloat16),
            pltpu.VMEM((SPAN, 8, rows), jnp.int32),
            pltpu.VMEM((rows, window), jnp.float32),
            pltpu.VMEM((rows, q_width), jnp.bfloat16),
            pltpu.SemaphoreType.DMA((6, 2 * cuts + 1, n)),
            pltpu.SemaphoreType.DMA((2 * cuts + 1, n)),
            pltpu.SemaphoreType.DMA((SPAN - 1, 3)),
            pltpu.SemaphoreType.DMA((SPAN - 1, 3)),
        ],
        compiler_params=pltpu.CompilerParams(
            collective_id=0, has_side_effects=True, vmem_limit_bytes=56 * 2**20),
        cost_estimate=pl.CostEstimate(
            flops=2 * rows * q_width * (2 * window + width),
            bytes_accessed=4 * rows * width, transcendentals=rows * window * HEADS),
    )(queries, keys, values, seg_row, seg_col, out_weight)


def solution(mesh):
    in_specs = (
        P(("groups", "seq"), None),
        P(("groups", "seq"), None),
        P(("groups", "seq"), None),
        P(("groups", "seq")),
        P("seq", None),
    )
    out_specs = P(("groups", "seq"), None)
    return jax.shard_map(body, mesh=mesh, in_specs=in_specs, out_specs=out_specs, check_vma=False)
```

```python
import functools
import math

import jax
import jax.numpy as jnp
from jax import lax
from jax.experimental import pallas as pl
from jax.experimental.pallas import tpu as pltpu
from jax.sharding import PartitionSpec as P

HEADS = 16
KV_HEADS = 4
HEAD = 128
SPAN = 4
CORES = 2
UP_A, DOWN_A, UP_B, DOWN_B, ACROSS, SIBLING = range(6)


def grid_of(n):
    chips = n // CORES
    b = max(d for d in range(1, chips + 1) if chips % d == 0 and d * d <= chips)
    return chips // b, b


def kernel(n, A, B, wx, tile,
           q_ref, k_ref, v_ref, seg_row_ref, seg_col_ref, w_ref, out_ref,
           W, kwin, vwin, swin, bias, att,
           send, recv, kv_send, kv_recv):
    rows = q_ref.shape[0]
    depth = w_ref.shape[0]
    width = w_ref.shape[1]
    g = lax.axis_index("groups")
    i = lax.axis_index("seq")
    c = lax.rem(i, CORES)
    chip = i // CORES
    b = lax.rem(chip, B)
    a = chip // B

    def index(a_, b_, c_):
        return (a_ * B + b_) * CORES + c_

    half = (width - 2 * wx) // (2 * tile) * tile
    MINE, BOTH, TURNED, THEIRS = (0,), (1,), (2,), (3,)
    widths = (wx, width - 2 * wx - half, half, wx)
    starts = (g * wx, 2 * wx, width - half, (1 - g) * wx)
    number = (g, 2, 3, 1 - g)

    def move(p, s, way, device):
        view = W.at[pl.ds(pl.multiple_of(s * depth, depth), depth),
                    pl.ds(pl.multiple_of(starts[p], 128), widths[p])]
        return pltpu.make_async_remote_copy(
            src_ref=view, dst_ref=view,
            send_sem=send.at[way, p, s], recv_sem=recv.at[number[p], s],
            device_id=device, device_id_type=pl.DeviceIdType.MESH)

    def act(copy, mode):
        if mode == "start":
            copy.start()
        else:
            copy.wait_send()

    up_a = (g, index(a + 1, b, c))
    down_a = (g, index(a - 1, b, c))
    up_b = (g, index(a, b + 1, c))
    down_b = (g, index(a, b - 1, c))
    across = (1 - g, i)
    sibling = (g, index(a, b, 1 - c))

    def along_b(p, s, mode):
        pl.when(b + 1 < B)(lambda: act(move(p, s, UP_B, up_b), mode))
        pl.when(b > 0)(lambda: act(move(p, s, DOWN_B, down_b), mode))

    def arrive(p, s, mode):
        if mode == "start":
            move(p, s, SIBLING, sibling).wait_recv()

    def own(pieces, mode):
        for p in pieces:
            pl.when(a + 1 < A)(lambda: act(move(p, i, UP_A, up_a), mode))
            pl.when(a > 0)(lambda: act(move(p, i, DOWN_A, down_a), mode))
            along_b(p, i, mode)
            act(move(p, i, SIBLING, sibling), mode)

    def from_a(p, t, mode):
        def take(a_, way, device, more):
            s = index(a_, b, c)
            arrive(p, s, mode)
            pl.when(more)(lambda: act(move(p, s, way, device), mode))
            along_b(p, s, mode)
            if p in MINE:
                act(move(p, s, ACROSS, across), mode)
            act(move(p, s, SIBLING, sibling), mode)

        pl.when(a - t >= 0)(lambda: take(a - t, UP_A, up_a, a + 1 < A))
        pl.when(a + t < A)(lambda: take(a + t, DOWN_A, down_a, a > 0))

    def from_b(p, t, mode):
        def take(a_, b_, way, device, more):
            s = index(a_, b_, c)
            arrive(p, s, mode)
            pl.when(more)(lambda: act(move(p, s, way, device), mode))
            if p in MINE:
                act(move(p, s, ACROSS, across), mode)
            act(move(p, s, SIBLING, sibling), mode)

        def column(a_):
            def step(u, carry):
                pl.when(b - u >= 0)(lambda: take(a_, b - u, UP_B, up_b, b + 1 < B))
                pl.when(b + u < B)(lambda: take(a_, b + u, DOWN_B, down_b, b > 0))
                return carry

            lax.fori_loop(1, B, step, 0)

        if t == 0:
            column(a)
        else:
            pl.when(a - t >= 0)(lambda: column(a - t))
            pl.when(a + t < A)(lambda: column(a + t))

    def turned(p, t, mode):
        def take(a_, b_, ways):
            s = index(a_, b_, c)
            arrive(p, s, mode)
            for way, device, more in ways:
                pl.when(more)(functools.partial(
                    lambda way, device: act(move(p, s, way, device), mode), way, device))
            act(move(p, s, SIBLING, sibling), mode)

        up = (UP_A, up_a, a + 1 < A)
        down = (DOWN_A, down_a, a > 0)

        def step(u, carry):
            if t == 0:
                pl.when(b - u >= 0)(lambda: take(
                    a, b - u, ((UP_B, up_b, b + 1 < B), up, down)))
                pl.when(b + u < B)(lambda: take(
                    a, b + u, ((DOWN_B, down_b, b > 0), up, down)))
            else:
                pl.when(a - t >= 0)(lambda: take(a - t, u, (up,)))
                pl.when(a + t < A)(lambda: take(a + t, u, (down,)))
            return carry

        lax.fori_loop(1 if t == 0 else 0, B, step, 0)

    def from_across(p, t, mode):
        def column(a_):
            def step(b_, carry):
                s = index(a_, b_, c)

                @pl.when(s != i)
                def _():
                    arrive(p, s, mode)
                    act(move(p, s, SIBLING, sibling), mode)

                return carry

            lax.fori_loop(0, B, step, 0)

        if t == 0:
            column(a)
        else:
            pl.when(a - t >= 0)(lambda: column(a - t))
            pl.when(a + t < A)(lambda: column(a + t))

    last = SPAN - 1
    routes = ((last, 1, (g, lax.rem(i + 2, n))),
              (1, 2 * c, sibling),
              (last, 2 - 2 * c, (g, lax.rem(i + 1 + 2 * c, n))))

    def kv_copies(way):
        mine, theirs, to = routes[way]
        return [
            pltpu.make_async_remote_copy(
                src_ref=ref.at[mine], dst_ref=ref.at[theirs],
                send_sem=kv_send.at[way, m], recv_sem=kv_recv.at[theirs, m],
                device_id=to, device_id_type=pl.DeviceIdType.MESH)
            for m, ref in enumerate((kwin, vwin, swin))]

    barrier = pltpu.get_barrier_semaphore()

    def greet(device):
        pl.semaphore_signal(barrier, inc=1, device_id=device,
                            device_id_type=pl.DeviceIdType.MESH)

    pl.when(a + 1 < A)(lambda: greet(up_a))
    pl.when(a > 0)(lambda: greet(down_a))
    pl.when(b + 1 < B)(lambda: greet(up_b))
    pl.when(b > 0)(lambda: greet(down_b))
    greet(across)
    greet(sibling)
    for d in range(1, SPAN):
        greet((g, lax.rem(i + d, n)))
        greet((g, lax.rem(i + n - d, n)))
    W[pl.ds(pl.multiple_of(i * depth, depth), depth), :] = w_ref[...]
    kwin[SPAN - 1] = k_ref[...]
    vwin[SPAN - 1] = v_ref[...]
    swin[SPAN - 1] = seg_row_ref[...]
    expected = (2 + 2 * (SPAN - 1)
                + jnp.where(a + 1 < A, 1, 0) + jnp.where(a > 0, 1, 0)
                + jnp.where(b + 1 < B, 1, 0) + jnp.where(b > 0, 1, 0))
    pl.semaphore_wait(barrier, expected)

    own(MINE, "start")
    for way in (0, 2):
        for copy in kv_copies(way):
            copy.start()
    own(BOTH + TURNED, "start")
    for p in THEIRS:
        move(p, i, SIBLING, sibling).start()

    def slot(j):
        return [
            pltpu.make_async_remote_copy(
                src_ref=ref.at[last], dst_ref=ref.at[j],
                send_sem=kv_send.at[0, m], recv_sem=kv_recv.at[j, m],
                device_id=sibling, device_id_type=pl.DeviceIdType.MESH)
            for m, ref in enumerate((kwin, vwin, swin))]

    def mask():
        for j in range(SPAN):
            row = lax.broadcasted_iota(jnp.int32, (rows, rows), 0)
            col = lax.broadcasted_iota(jnp.int32, (rows, rows), 1) + (j - SPAN + 1) * rows
            live = (seg_col_ref[:, 0:1] == swin[j, 0:1, :]) & (col <= row) & (col + i * rows >= 0)
            bias[:, j * rows:(j + 1) * rows] = jnp.where(live, 0.0, -jnp.inf)

    factor = HEAD ** -0.5 * math.log2(math.e)
    group = HEADS // KV_HEADS

    def attend(kv):
        lanes = slice(kv * HEAD, (kv + 1) * HEAD)
        keys = jnp.concatenate([kwin[j, :, lanes] for j in range(SPAN)], axis=0)
        vals = jnp.concatenate([vwin[j, :, lanes] for j in range(SPAN)], axis=0)
        for m in range(group):
            h = kv * group + m
            q = q_ref[:, h * HEAD:(h + 1) * HEAD]
            scores = lax.dot_general(q, keys, (((1,), (1,)), ((), ())),
                                     preferred_element_type=jnp.float32)
            scores = scores * factor + bias[...]
            top = jnp.max(scores, axis=-1, keepdims=True)
            weights = jnp.exp2(scores - top)
            total = jnp.sum(weights, axis=-1, keepdims=True)
            mix = jnp.dot(weights.astype(jnp.bfloat16), vals,
                          preferred_element_type=jnp.float32)
            att[:, h * HEAD:(h + 1) * HEAD] = (mix / total).astype(jnp.bfloat16)

    done = 0
    for t in range(A):
        if t > 0:
            for p in MINE + BOTH:
                from_a(p, t, "start")
        for p in MINE + TURNED + BOTH:
            if p in TURNED:
                turned(p, t, "start")
            else:
                from_b(p, t, "start")
        if t == 0:
            for copy in slot(1):
                copy.wait_recv()
            for copy in kv_copies(1):
                copy.start()
        if t == 1:
            for j in (0, 2):
                for copy in slot(j):
                    copy.wait_recv()
            mask()
        if t > 0:
            for p in THEIRS:
                from_across(p, t - 1, "start")
            if done < KV_HEADS:
                attend(done)
                done += 1
    for kv in range(done, KV_HEADS):
        attend(kv)

    def project(p):
        def landed(m, carry):
            move(p, m * CORES + 1 - c, SIBLING, sibling).wait_recv()
            return carry

        lax.fori_loop(0, n // CORES, landed, 0)

        def one(m, carry):
            lanes = pl.ds(pl.multiple_of(starts[p] + m * tile, 128), tile)
            out_ref[:, lanes] = jnp.dot(
                att[...], W[:, lanes], preferred_element_type=jnp.float32
            ).astype(out_ref.dtype)
            return carry

        lax.fori_loop(0, widths[p] // tile, one, 0)

    for p in MINE:
        project(p)
    for p in THEIRS:
        from_across(p, A - 1, "start")
    for p in BOTH + TURNED + THEIRS:
        project(p)

    own(MINE + BOTH + TURNED, "wait")
    for p in THEIRS:
        move(p, i, SIBLING, sibling).wait_send()
    for t in range(A):
        for p in MINE + BOTH:
            if t > 0:
                from_a(p, t, "wait")
            from_b(p, t, "wait")
        for p in TURNED:
            turned(p, t, "wait")
        for p in THEIRS:
            from_across(p, t, "wait")
    for way in range(3):
        for copy in kv_copies(way):
            copy.wait_send()


def body(queries, keys, values, segment, out_weight):
    rows, q_width = queries.shape
    kv_width = keys.shape[1]
    n = lax.axis_size("seq")
    width = out_weight.shape[1]
    A, B = grid_of(n)
    tile = math.gcd(width, 512)
    wx = width * 3 // 8 // tile * tile
    seg_row = jnp.broadcast_to(segment[None, :], (8, rows))
    seg_col = jnp.broadcast_to(segment[:, None], (rows, 128))
    vmem = pl.BlockSpec(memory_space=pltpu.VMEM)
    window = rows * SPAN
    return pl.pallas_call(
        functools.partial(kernel, n, A, B, wx, tile),
        out_shape=jax.ShapeDtypeStruct((rows, width), jnp.bfloat16),
        in_specs=[vmem] * 6,
        out_specs=vmem,
        scratch_shapes=[
            pltpu.VMEM((out_weight.shape[0] * n, width), jnp.bfloat16),
            pltpu.VMEM((SPAN, rows, kv_width), jnp.bfloat16),
            pltpu.VMEM((SPAN, rows, kv_width), jnp.bfloat16),
            pltpu.VMEM((SPAN, 8, rows), jnp.int32),
            pltpu.VMEM((rows, window), jnp.float32),
            pltpu.VMEM((rows, q_width), jnp.bfloat16),
            pltpu.SemaphoreType.DMA((6, 4, n)),
            pltpu.SemaphoreType.DMA((4, n)),
            pltpu.SemaphoreType.DMA((SPAN - 1, 3)),
            pltpu.SemaphoreType.DMA((SPAN - 1, 3)),
        ],
        compiler_params=pltpu.CompilerParams(
            collective_id=0, has_side_effects=True, vmem_limit_bytes=56 * 2**20),
        cost_estimate=pl.CostEstimate(
            flops=2 * rows * q_width * (2 * window + width),
            bytes_accessed=4 * rows * width, transcendentals=rows * window * HEADS),
    )(queries, keys, values, seg_row, seg_col, out_weight)


def solution(mesh):
    in_specs = (
        P(("groups", "seq"), None),
        P(("groups", "seq"), None),
        P(("groups", "seq"), None),
        P(("groups", "seq")),
        P("seq", None),
    )
    out_specs = P(("groups", "seq"), None)
    return jax.shard_map(body, mesh=mesh, in_specs=in_specs, out_specs=out_specs, check_vma=False)
```

```python
import functools
import math

import jax
import jax.numpy as jnp
from jax import lax
from jax.experimental import pallas as pl
from jax.experimental.pallas import tpu as pltpu
from jax.sharding import PartitionSpec as P

HEADS = 16
KV_HEADS = 4
HEAD = 128
SPAN = 4
CORES = 2
UP_A, DOWN_A, UP_B, DOWN_B, ACROSS, SIBLING = range(6)


def grid_of(n):
    chips = n // CORES
    b = max(d for d in range(1, chips + 1) if chips % d == 0 and d * d <= chips)
    return chips // b, b


def kernel(n, A, B, wx, tile,
           q_ref, k_ref, v_ref, seg_row_ref, seg_col_ref, w_ref, out_ref,
           W, kwin, vwin, swin, bias, att,
           send, recv, kv_send, kv_recv):
    rows = q_ref.shape[0]
    depth = w_ref.shape[0]
    width = w_ref.shape[1]
    g = lax.axis_index("groups")
    i = lax.axis_index("seq")
    c = lax.rem(i, CORES)
    chip = i // CORES
    b = lax.rem(chip, B)
    a = chip // B

    def index(a_, b_, c_):
        return (a_ * B + b_) * CORES + c_

    half = (width - 2 * wx) // (2 * tile) * tile
    MINE, BOTH, TURNED, THEIRS = (0,), (1,), (2,), (3,)
    widths = (wx, width - 2 * wx - half, half, wx)
    starts = (g * wx, 2 * wx, width - half, (1 - g) * wx)
    number = (g, 2, 3, 1 - g)

    def move(p, s, way, device):
        view = W.at[pl.ds(pl.multiple_of(s * depth, depth), depth),
                    pl.ds(pl.multiple_of(starts[p], 128), widths[p])]
        return pltpu.make_async_remote_copy(
            src_ref=view, dst_ref=view,
            send_sem=send.at[way, p, s], recv_sem=recv.at[number[p], s],
            device_id=device, device_id_type=pl.DeviceIdType.MESH)

    def act(copy, mode):
        if mode == "start":
            copy.start()
        else:
            copy.wait_send()

    up_a = (g, index(a + 1, b, c))
    down_a = (g, index(a - 1, b, c))
    up_b = (g, index(a, b + 1, c))
    down_b = (g, index(a, b - 1, c))
    across = (1 - g, i)
    sibling = (g, index(a, b, 1 - c))

    def along_b(p, s, mode):
        pl.when(b + 1 < B)(lambda: act(move(p, s, UP_B, up_b), mode))
        pl.when(b > 0)(lambda: act(move(p, s, DOWN_B, down_b), mode))

    def arrive(p, s, mode):
        if mode == "start":
            move(p, s, SIBLING, sibling).wait_recv()

    def own(pieces, mode):
        for p in pieces:
            pl.when(a + 1 < A)(lambda: act(move(p, i, UP_A, up_a), mode))
            pl.when(a > 0)(lambda: act(move(p, i, DOWN_A, down_a), mode))
            along_b(p, i, mode)
            act(move(p, i, SIBLING, sibling), mode)

    def from_a(p, t, mode):
        def take(a_, way, device, more):
            s = index(a_, b, c)
            arrive(p, s, mode)
            pl.when(more)(lambda: act(move(p, s, way, device), mode))
            along_b(p, s, mode)
            if p in MINE:
                act(move(p, s, ACROSS, across), mode)
            act(move(p, s, SIBLING, sibling), mode)

        pl.when(a - t >= 0)(lambda: take(a - t, UP_A, up_a, a + 1 < A))
        pl.when(a + t < A)(lambda: take(a + t, DOWN_A, down_a, a > 0))

    def from_b(p, t, mode):
        def take(a_, b_, way, device, more):
            s = index(a_, b_, c)
            arrive(p, s, mode)
            pl.when(more)(lambda: act(move(p, s, way, device), mode))
            if p in MINE:
                act(move(p, s, ACROSS, across), mode)
            act(move(p, s, SIBLING, sibling), mode)

        def column(a_):
            def step(u, carry):
                pl.when(b - u >= 0)(lambda: take(a_, b - u, UP_B, up_b, b + 1 < B))
                pl.when(b + u < B)(lambda: take(a_, b + u, DOWN_B, down_b, b > 0))
                return carry

            lax.fori_loop(1, B, step, 0)

        if t == 0:
            column(a)
        else:
            pl.when(a - t >= 0)(lambda: column(a - t))
            pl.when(a + t < A)(lambda: column(a + t))

    def turned(p, t, mode):
        def take(a_, b_, ways):
            s = index(a_, b_, c)
            arrive(p, s, mode)
            for way, device, more in ways:
                pl.when(more)(functools.partial(
                    lambda way, device: act(move(p, s, way, device), mode), way, device))
            act(move(p, s, SIBLING, sibling), mode)

        up = (UP_A, up_a, a + 1 < A)
        down = (DOWN_A, down_a, a > 0)

        def step(u, carry):
            if t == 0:
                pl.when(b - u >= 0)(lambda: take(
                    a, b - u, ((UP_B, up_b, b + 1 < B), up, down)))
                pl.when(b + u < B)(lambda: take(
                    a, b + u, ((DOWN_B, down_b, b > 0), up, down)))
            else:
                pl.when(a - t >= 0)(lambda: take(a - t, u, (up,)))
                pl.when(a + t < A)(lambda: take(a + t, u, (down,)))
            return carry

        lax.fori_loop(1 if t == 0 else 0, B, step, 0)

    def from_across(p, t, mode):
        def column(a_):
            def step(b_, carry):
                s = index(a_, b_, c)

                @pl.when(s != i)
                def _():
                    arrive(p, s, mode)
                    act(move(p, s, SIBLING, sibling), mode)

                return carry

            lax.fori_loop(0, B, step, 0)

        if t == 0:
            column(a)
        else:
            pl.when(a - t >= 0)(lambda: column(a - t))
            pl.when(a + t < A)(lambda: column(a + t))

    last = SPAN - 1
    routes = ((last, 1, (g, lax.rem(i + 2, n))),
              (1, 2 * c, sibling),
              (last, 2 - 2 * c, (g, lax.rem(i + 1 + 2 * c, n))))

    def kv_copies(way):
        mine, theirs, to = routes[way]
        return [
            pltpu.make_async_remote_copy(
                src_ref=ref.at[mine], dst_ref=ref.at[theirs],
                send_sem=kv_send.at[way, m], recv_sem=kv_recv.at[theirs, m],
                device_id=to, device_id_type=pl.DeviceIdType.MESH)
            for m, ref in enumerate((kwin, vwin, swin))]

    barrier = pltpu.get_barrier_semaphore()

    def greet(device):
        pl.semaphore_signal(barrier, inc=1, device_id=device,
                            device_id_type=pl.DeviceIdType.MESH)

    pl.when(a + 1 < A)(lambda: greet(up_a))
    pl.when(a > 0)(lambda: greet(down_a))
    pl.when(b + 1 < B)(lambda: greet(up_b))
    pl.when(b > 0)(lambda: greet(down_b))
    greet(across)
    greet(sibling)
    for d in range(1, SPAN):
        greet((g, lax.rem(i + d, n)))
        greet((g, lax.rem(i + n - d, n)))
    W[pl.ds(pl.multiple_of(i * depth, depth), depth), :] = w_ref[...]
    kwin[SPAN - 1] = k_ref[...]
    vwin[SPAN - 1] = v_ref[...]
    swin[SPAN - 1] = seg_row_ref[...]
    expected = (2 + 2 * (SPAN - 1)
                + jnp.where(a + 1 < A, 1, 0) + jnp.where(a > 0, 1, 0)
                + jnp.where(b + 1 < B, 1, 0) + jnp.where(b > 0, 1, 0))
    pl.semaphore_wait(barrier, expected)

    own(MINE, "start")
    for way in (0, 2):
        for copy in kv_copies(way):
            copy.start()
    own(BOTH + TURNED, "start")
    for p in THEIRS:
        move(p, i, SIBLING, sibling).start()

    def slot(j):
        return [
            pltpu.make_async_remote_copy(
                src_ref=ref.at[last], dst_ref=ref.at[j],
                send_sem=kv_send.at[0, m], recv_sem=kv_recv.at[j, m],
                device_id=sibling, device_id_type=pl.DeviceIdType.MESH)
            for m, ref in enumerate((kwin, vwin, swin))]

    def mask():
        for j in range(SPAN):
            row = lax.broadcasted_iota(jnp.int32, (rows, rows), 0)
            col = lax.broadcasted_iota(jnp.int32, (rows, rows), 1) + (j - SPAN + 1) * rows
            live = (seg_col_ref[:, 0:1] == swin[j, 0:1, :]) & (col <= row) & (col + i * rows >= 0)
            bias[:, j * rows:(j + 1) * rows] = jnp.where(live, 0.0, -jnp.inf)

    factor = HEAD ** -0.5 * math.log2(math.e)
    group = HEADS // KV_HEADS

    def attend(kv):
        lanes = slice(kv * HEAD, (kv + 1) * HEAD)
        keys = jnp.concatenate([kwin[j, :, lanes] for j in range(SPAN)], axis=0)
        vals = jnp.concatenate([vwin[j, :, lanes] for j in range(SPAN)], axis=0)
        for m in range(group):
            h = kv * group + m
            q = q_ref[:, h * HEAD:(h + 1) * HEAD]
            scores = lax.dot_general(q, keys, (((1,), (1,)), ((), ())),
                                     preferred_element_type=jnp.float32)
            scores = scores * factor + bias[...]
            top = jnp.max(scores, axis=-1, keepdims=True)
            weights = jnp.exp2(scores - top)
            total = jnp.sum(weights, axis=-1, keepdims=True)
            mix = jnp.dot(weights.astype(jnp.bfloat16), vals,
                          preferred_element_type=jnp.float32)
            att[:, h * HEAD:(h + 1) * HEAD] = (mix / total).astype(jnp.bfloat16)

    done = 0
    for t in range(A):
        if t > 0:
            for p in MINE + BOTH:
                from_a(p, t, "start")
        for p in MINE + TURNED + BOTH if t == 0 else TURNED + MINE + BOTH:
            if p in TURNED:
                turned(p, t, "start")
            else:
                from_b(p, t, "start")
        if t == 0:
            for copy in slot(1):
                copy.wait_recv()
            for copy in kv_copies(1):
                copy.start()
        if t == 1:
            for j in (0, 2):
                for copy in slot(j):
                    copy.wait_recv()
            mask()
        if t > 0:
            if done < KV_HEADS:
                attend(done)
                done += 1
            for p in THEIRS:
                from_across(p, t - 1, "start")
    for kv in range(done, KV_HEADS):
        attend(kv)

    def project(p):
        def landed(m, carry):
            move(p, m * CORES + 1 - c, SIBLING, sibling).wait_recv()
            return carry

        lax.fori_loop(0, n // CORES, landed, 0)

        def one(m, carry):
            lanes = pl.ds(pl.multiple_of(starts[p] + m * tile, 128), tile)
            out_ref[:, lanes] = jnp.dot(
                att[...], W[:, lanes], preferred_element_type=jnp.float32
            ).astype(out_ref.dtype)
            return carry

        lax.fori_loop(0, widths[p] // tile, one, 0)

    for p in MINE:
        project(p)
    for p in THEIRS:
        from_across(p, A - 1, "start")
    for p in BOTH + TURNED + THEIRS:
        project(p)

    own(MINE + BOTH + TURNED, "wait")
    for p in THEIRS:
        move(p, i, SIBLING, sibling).wait_send()
    for t in range(A):
        for p in MINE + BOTH:
            if t > 0:
                from_a(p, t, "wait")
            from_b(p, t, "wait")
        for p in TURNED:
            turned(p, t, "wait")
        for p in THEIRS:
            from_across(p, t, "wait")
    for way in range(3):
        for copy in kv_copies(way):
            copy.wait_send()


def body(queries, keys, values, segment, out_weight):
    rows, q_width = queries.shape
    kv_width = keys.shape[1]
    n = lax.axis_size("seq")
    width = out_weight.shape[1]
    A, B = grid_of(n)
    tile = math.gcd(width, 512)
    wx = width * 3 // 8 // tile * tile
    seg_row = jnp.broadcast_to(segment[None, :], (8, rows))
    seg_col = jnp.broadcast_to(segment[:, None], (rows, 128))
    vmem = pl.BlockSpec(memory_space=pltpu.VMEM)
    window = rows * SPAN
    return pl.pallas_call(
        functools.partial(kernel, n, A, B, wx, tile),
        out_shape=jax.ShapeDtypeStruct((rows, width), jnp.bfloat16),
        in_specs=[vmem] * 6,
        out_specs=vmem,
        scratch_shapes=[
            pltpu.VMEM((out_weight.shape[0] * n, width), jnp.bfloat16),
            pltpu.VMEM((SPAN, rows, kv_width), jnp.bfloat16),
            pltpu.VMEM((SPAN, rows, kv_width), jnp.bfloat16),
            pltpu.VMEM((SPAN, 8, rows), jnp.int32),
            pltpu.VMEM((rows, window), jnp.float32),
            pltpu.VMEM((rows, q_width), jnp.bfloat16),
            pltpu.SemaphoreType.DMA((6, 4, n)),
            pltpu.SemaphoreType.DMA((4, n)),
            pltpu.SemaphoreType.DMA((SPAN - 1, 3)),
            pltpu.SemaphoreType.DMA((SPAN - 1, 3)),
        ],
        compiler_params=pltpu.CompilerParams(
            collective_id=0, has_side_effects=True, vmem_limit_bytes=56 * 2**20),
        cost_estimate=pl.CostEstimate(
            flops=2 * rows * q_width * (2 * window + width),
            bytes_accessed=4 * rows * width, transcendentals=rows * window * HEADS),
    )(queries, keys, values, seg_row, seg_col, out_weight)


def solution(mesh):
    in_specs = (
        P(("groups", "seq"), None),
        P(("groups", "seq"), None),
        P(("groups", "seq"), None),
        P(("groups", "seq")),
        P("seq", None),
    )
    out_specs = P(("groups", "seq"), None)
    return jax.shard_map(body, mesh=mesh, in_specs=in_specs, out_specs=out_specs, check_vma=False)
```
